256 devices in a mesh: freq: 16 (over y, x), rows: 16 (over z, core).
Axes of the slice: x: 4, y: 4, z: 8, core: 2. Of those that a mesh axis runs over, the one named last changes fastest.
Arguments:
- basis: float32 [64, 64, 2, 128, 256], P('freq', 'rows'), parts along dimension 0, may hold values from -40 to 40
- near_blocks: bfloat16 [512, 32, 128, 128], P('rows', 'freq'), parts along dimension 1, may hold values from -0.125 to 0.125
- near_pairs: int32 [512, 2], P('rows'), may hold values from 0 to 63, as said below
- bfly_weights: bfloat16 [96, 64, 4, 128, 128], P('freq', 'rows'), parts along dimension 0, may hold values from -0.25 to 0.25
- partner_local: int32 [6, 64], P(None, 'rows'), may hold values from 0 to 3
Outputs:
- next_vector: float32 [64, 32, 128, 256], P('rows', 'freq'), parts along dimension 1
- coeffs: float32 [80, 2, 256], P('freq'), parts along dimension 0
The draws below stay inside these ranges and needn't reach their ends.
There are 16 independent parts, one for each index of `freq`. The reference program is written for one: setup_inputs(seed, part) draws one part's arguments, and reference() takes and returns one part's arrays. A program takes and returns all parts, laid end to end along the dimension named above; an argument that names none is the same for every part. Nothing has to cross between parts.
Inputs may be any that keep to these rules, and one draw needn't show every extreme that they name: `near_pairs`: the first 28 slots of each device hold blocks of that device's own block rows; the other 4 hold blocks shipped to it, of any block row. A slot's column block lies within 2 blocks of its row block.
All inputs are finite; a program needn't handle non-finite values.
Results may differ from the reference program's by a relative error of at most 0.0065.
Values may be sent and summed in bfloat16 or wider, within the bound.
No kernel may reach another device: no remote copies, remote signals or barrier semaphores. Data moves between devices by JAX's collectives and lax.ppermute only.
A program may use at most 192 MiB of HBM per device.

```python
import jax
import jax.numpy as jnp
from jax import lax

BS = 128
LEVELS = 6
R = 256
KRYLOV = 4
OWN = 28
REACH = 2
NBLK = 64
NB_DEV = 4
SLOTS = 32
SLOTS_ALL = 512


def draw_basis(key, part):
    key = jax.random.fold_in(key, 11)
    first, second = jax.random.split(key, 2)
    shape_one = (NBLK, 2, BS, R)
    common = jax.random.normal(first, shape_one, jnp.float32)
    others = jax.random.normal(second, (KRYLOV,) + shape_one, jnp.float32)
    return jnp.clip(0.6 * common + 0.8 * others, -6.0, 6.0)


def draw_near_pairs(key, part):
    key = jax.random.fold_in(key, 23)
    first, second, third = jax.random.split(key, 3)
    slot_ids = jnp.arange(SLOTS_ALL, dtype=jnp.int32)
    owner = slot_ids // SLOTS
    within = slot_ids % SLOTS
    own_row = owner * NB_DEV + jax.random.randint(first, (SLOTS_ALL,), 0, NB_DEV, dtype=jnp.int32)
    any_row = jax.random.randint(second, (SLOTS_ALL,), 0, NBLK, dtype=jnp.int32)
    row_block = jnp.where(within < OWN, own_row, any_row)
    offset = jax.random.randint(third, (SLOTS_ALL,), -REACH, REACH + 1, dtype=jnp.int32)
    col_block = jnp.clip(row_block + offset, 0, NBLK - 1)
    return jnp.stack([row_block, col_block], axis=1).astype(jnp.int32)


def set_ends(entries, stream_key, least, high):
    spot = [jax.random.randint(jax.random.fold_in(stream_key, axis), (), 0, length) for axis, length in enumerate(entries.shape)]
    longest = entries.shape.index(max(entries.shape))
    beside = spot[:longest] + [(spot[longest] + 1) % entries.shape[longest]] + spot[longest + 1:]
    return entries.at[tuple(spot)].set(least).at[tuple(beside)].set(high)


def shard_levels(own_key, extent, cuts, low, high):
    def one(dim, blocks):
        draws = jax.random.uniform(jax.random.fold_in(jax.random.fold_in(own_key, 6), dim), (blocks,), jnp.float32, low / len(cuts), high / len(cuts))
        return jnp.repeat(jnp.exp(draws), extent[dim] // blocks).reshape((-1,) + (1,) * (len(extent) - dim - 1))

    factor_of = one(*cuts[0])
    for cut in cuts[1:]:
        factor_of = factor_of * one(*cut)
    return factor_of


def normal_values(own_key, dims, deviation, most, pieces=(), held_as=jnp.bfloat16):
    result = deviation * jax.random.normal(own_key, dims, jnp.float32)
    if pieces:
        result = result * shard_levels(own_key, dims, pieces, -0.22, 0.18)
    return jnp.clip(result, -most, most).astype(held_as)


def setup_inputs(seed: int = 0, part: int = 0) -> dict:
    key_of = jax.random.split(jax.random.key(seed), 6)
    part_splits = jax.random.split(jax.random.fold_in(key_of[5], part), 6)
    return {
        "basis": draw_basis(jax.random.fold_in(jax.random.fold_in(key_of[5], part), 71), part),
        "near_blocks": normal_values(part_splits[1], (SLOTS_ALL, 2, BS, BS), (2 * BS * SLOTS // NB_DEV) ** -0.5, 0.125, ((0, 16),)),
        "near_pairs": draw_near_pairs(jax.random.fold_in(key_of[5], 71), part),
        "bfly_weights": normal_values(part_splits[3], (LEVELS, NBLK, 4, BS, BS), (4 * BS) ** -0.5, 0.25, ((1, 16),)),
        "partner_local": set_ends(jax.random.randint(key_of[4], (LEVELS, NBLK), 0, NB_DEV), jax.random.fold_in(key_of[4], 1), 0, NB_DEV - 1).astype(jnp.int32),
    }


def complex_blocks(blocks, vectors):
    zb = blocks.astype(jnp.float32)
    xb = vectors.astype(jnp.float32)

    def single(left, right):
        return jnp.einsum('sij,sjr->sir', left, right, precision=lax.Precision.HIGHEST)
    real = single(zb[:, 0], xb[:, 0]) - single(zb[:, 1], xb[:, 1])
    imag = single(zb[:, 0], xb[:, 1]) + single(zb[:, 1], xb[:, 0])
    return jnp.stack([real, imag], axis=1)

def reference(basis, near_blocks, near_pairs, bfly_weights, partner_local):
    last = basis[KRYLOV - 1]
    xv = last.astype(jnp.bfloat16)
    rows_of = near_pairs[:, 0].astype(jnp.int32)
    cols_of = near_pairs[:, 1].astype(jnp.int32)
    prods = complex_blocks(near_blocks, xv[cols_of])
    near = jax.ops.segment_sum(prods, rows_of, num_segments=NBLK)
    local_levels = NB_DEV.bit_length() - 1
    block_ids = jnp.arange(NBLK, dtype=jnp.int32)
    section = xv
    for level in range(LEVELS):
        flip = 0 if level < local_levels else 1 << level - local_levels
        source = jnp.bitwise_xor(block_ids // NB_DEV, flip) * NB_DEV + partner_local[level].astype(jnp.int32)
        weights = bfly_weights[level]
        section = (complex_blocks(weights[:, 0:2], section) + complex_blocks(weights[:, 2:4], section[source])).astype(jnp.bfloat16)
    product = last + near + section.astype(jnp.float32)
    scale = 1.0 / (NBLK * BS)
    basis_re = basis[:, :, 0]
    basis_im = basis[:, :, 1]
    prod_re = product[:, 0]
    prod_im = product[:, 1]
    proj_re = lax.optimization_barrier(jnp.sum(basis_re * prod_re + basis_im * prod_im, axis=(1, 2))) * scale
    proj_im = lax.optimization_barrier(jnp.sum(basis_re * prod_im - basis_im * prod_re, axis=(1, 2))) * scale
    orth_re = prod_re - lax.optimization_barrier(jnp.sum(basis_re * proj_re[:, None, None, :] - basis_im * proj_im[:, None, None, :], axis=0))
    orth_im = prod_im - lax.optimization_barrier(jnp.sum(basis_re * proj_im[:, None, None, :] + basis_im * proj_re[:, None, None, :], axis=0))
    mean_square = lax.optimization_barrier(jnp.sum(orth_re * orth_re + orth_im * orth_im, axis=(0, 1))) * scale
    norm_value = jnp.sqrt(mean_square + 1e-06)
    next_vector = jnp.stack([orth_re, orth_im], axis=1) / norm_value
    head = jnp.stack([proj_re, proj_im], axis=1)
    tail = jnp.stack([norm_value, jnp.zeros_like(norm_value)], axis=0)[None]
    coeffs = jnp.concatenate([head, tail], axis=0)
    return (next_vector, coeffs)
```

```python
import functools

import jax
import jax.numpy as jnp
from jax import lax
from jax.experimental import pallas as pl
from jax.experimental.pallas import tpu as pltpu
from jax.sharding import PartitionSpec as P

LEVELS = 6
REACH = 2
OWN = 28
CHUNKS = 2
F32 = jnp.float32
BF16 = jnp.bfloat16
VMEM = pl.BlockSpec(memory_space=pltpu.VMEM)
SMEM = pl.BlockSpec(memory_space=pltpu.SMEM)


def call(kernel, outs, in_specs, scratch=(), flops=0, bytes_accessed=0, limit=32):
    return pl.pallas_call(
        kernel,
        out_shape=outs,
        grid=(1,),
        in_specs=in_specs,
        out_specs=jax.tree.map(lambda _: VMEM, outs),
        scratch_shapes=list(scratch),
        compiler_params=pltpu.CompilerParams(vmem_limit_bytes=limit * 2**20),
        cost_estimate=pl.CostEstimate(flops=flops, bytes_accessed=bytes_accessed, transcendentals=0),
    )


def mixed(weights, own, picked):
    ur, ui, wr, wi = weights[0], weights[1], weights[2], weights[3]
    real = jnp.concatenate([ur, -ui, wr, -wi], axis=1)
    imag = jnp.concatenate([ui, ur, wi, wr], axis=1)
    left = jnp.concatenate([real, imag], axis=0)
    right = jnp.concatenate([own, picked], axis=0)
    return jnp.dot(left, right, preferred_element_type=F32)


def near_term(block, vector):
    zr, zi = block[0], block[1]
    left = jnp.concatenate(
        [jnp.concatenate([zr, -zi], axis=1), jnp.concatenate([zi, zr], axis=1)], axis=0
    )
    return jnp.dot(left, vector, preferred_element_type=F32)


def prep_kernel(partner, last, weights, low, high, *rest):
    sections, (zero, one) = rest[:-2], rest[-2:]
    blocks = last.shape[1]
    half = blocks // 2
    for b in range(blocks):
        zero[b] = last[0, b].reshape(zero.shape[1:]).astype(BF16)
    low[...] = zero[:half]
    high[...] = zero[half:]
    for b in range(blocks):
        one[b] = mixed(weights[0, b], zero[b], zero[partner[0, b]]).astype(BF16)
    for b in range(blocks):
        done = mixed(weights[1, b], one[b], one[partner[1, b]]).astype(BF16)
        width = done.shape[1] // len(sections)
        for c, section in enumerate(sections):
            section[b] = done[:, c * width : (c + 1) * width]


def level_kernel(level, partner, own, far, weights, out):
    for b in range(own.shape[0]):
        out[b] = mixed(weights[0, b], own[b], far[partner[level, b]]).astype(BF16)


def near_own_kernel(pairs, blocks, before, low, high, after, last, *rest):
    outs, (window, total) = rest[:-2], rest[-2:]
    rows = total.shape[0]
    half = rows // 2
    window[0:half] = before[...]
    window[half : 2 * half] = low[...]
    window[2 * half : 3 * half] = high[...]
    window[3 * half : 4 * half] = after[...]
    first = lax.axis_index("rows") * rows
    for b in range(rows):
        total[b] = last[0, b].reshape(total.shape[1:])

    def body(slot, carry):
        row = pairs[slot, 0] - first
        col = pairs[slot, 1] - first + REACH
        total[row] += near_term(blocks[slot], window[col])
        return carry

    lax.fori_loop(0, OWN, body, 0)
    width = total.shape[2] // len(outs)
    for c, out in enumerate(outs):
        out[...] = total[:, :, c * width : (c + 1) * width]


def near_shipped_kernel(pairs, blocks, before, low, high, after, *rest):
    window = rest[-1]
    count = (len(rest) - 1) // 2
    totals, outs = rest[:count], rest[count : 2 * count]
    rows = totals[0].shape[0]
    half = rows // 2
    entries = blocks.shape[2]
    window[0:half] = before[...]
    window[half : 2 * half] = low[...]
    window[2 * half : 3 * half] = high[...]
    window[3 * half : 4 * half] = after[...]
    first = lax.axis_index("rows") * rows
    for out, total in zip(outs, totals):
        out[...] = total[...]
    width = totals[0].shape[2]

    def body(slot, carry):
        row = pairs[slot, 0] - first
        col = pairs[slot, 1] - first + REACH

        @pl.when((row >= 0) & (row < rows))
        def _():
            block = (blocks[slot, 0:entries], blocks[slot, entries : 2 * entries])
            term = near_term(block, window[col])
            for c, out in enumerate(outs):
                out[row] += term[:, c * width : (c + 1) * width]

        return carry

    lax.fori_loop(0, blocks.shape[0], body, 0)


def gram_kernel(scale, basis, out):
    vectors, blocks = basis.shape[0], basis.shape[1]
    pairs = [(i, j) for i in range(vectors) for j in range(i, vectors)]
    out[...] = jnp.zeros_like(out)
    for b in range(blocks):
        at = 0
        for i, j in pairs:
            ir, ii, jr, ji = basis[i, b, 0], basis[i, b, 1], basis[j, b, 0], basis[j, b, 1]
            out[at : at + 1] += jnp.sum(ir * jr + ii * ji, axis=0, keepdims=True) * scale
            at += 1
            if i != j:
                out[at : at + 1] += jnp.sum(ir * ji - ii * jr, axis=0, keepdims=True) * scale
                at += 1


def project_kernel(level, scale, partner, own, far, weights, base, basis, gram, product, stats):
    vectors, blocks = basis.shape[0], basis.shape[1]
    entries = basis.shape[3]
    sums = [0.0] * (2 * vectors + 1)
    for b in range(blocks):
        section = mixed(weights[0, b], own[b], far[partner[level, b]]).astype(BF16)
        here = base[b] + section.astype(F32)
        product[b] = here
        pr, pi = here[:entries], here[entries:]
        for j in range(vectors):
            br, bi = basis[j, b, 0], basis[j, b, 1]
            sums[j] += jnp.sum(br * pr + bi * pi, axis=0, keepdims=True)
            sums[vectors + j] += jnp.sum(br * pi - bi * pr, axis=0, keepdims=True)
        sums[-1] += jnp.sum(pr * pr + pi * pi, axis=0, keepdims=True)
    used = len(sums)
    for k, value in enumerate(sums):
        stats[k : k + 1] = value * scale
    stats[used : used + gram.shape[0]] = gram[...]
    stats[used + gram.shape[0] :] = jnp.zeros_like(stats[used + gram.shape[0] :])


def finish_kernel(shared, basis, *rest):
    products, (following, coeffs) = rest[:-2], rest[-2:]
    vectors, blocks = basis.shape[0], basis.shape[1]
    entries = basis.shape[3]
    total = shared[0]
    for k in range(1, shared.shape[0]):
        total = total + shared[k]
    hr = [total[j : j + 1] for j in range(vectors)]
    hi = [total[vectors + j : vectors + j + 1] for j in range(vectors)]
    square = total[2 * vectors : 2 * vectors + 1]
    at = 2 * vectors + 1
    for i in range(vectors):
        for j in range(i, vectors):
            gr = total[at : at + 1]
            at += 1
            if i == j:
                square = square + (gr - 2.0) * (hr[i] * hr[i] + hi[i] * hi[i])
            else:
                gi = total[at : at + 1]
                at += 1
                square = square + 2.0 * (
                    gr * (hr[i] * hr[j] + hi[i] * hi[j]) - gi * (hr[i] * hi[j] - hi[i] * hr[j])
                )
    norm = jnp.sqrt(jnp.maximum(square, 0.0) + 1e-06)
    inverse = 1.0 / norm
    for j in range(vectors):
        coeffs[j, 0:1] = hr[j]
        coeffs[j, 1:2] = hi[j]
    coeffs[vectors, 0:1] = norm
    coeffs[vectors, 1:2] = jnp.zeros_like(norm)
    width = products[0].shape[2]
    for c, product in enumerate(products):
        cols = slice(c * width, (c + 1) * width)
        for b in range(blocks):
            real, imag = product[b, :entries], product[b, entries:]
            for j in range(vectors):
                br, bi = basis[j, b, 0, :, cols], basis[j, b, 1, :, cols]
                real = real - (br * hr[j][:, cols] - bi * hi[j][:, cols])
                imag = imag - (br * hi[j][:, cols] + bi * hr[j][:, cols])
            following[b, 0, :, cols] = real * inverse[:, cols]
            following[b, 1, :, cols] = imag * inverse[:, cols]


def swapped(value, mask):
    return lax.ppermute(value, "rows", [(i, i ^ mask) for i in range(lax.axis_size("rows"))])


def shifted(value, step):
    size = lax.axis_size("rows")
    return lax.ppermute(value, "rows", [(i, (i + step) % size) for i in range(size)])


def shards(basis, near_blocks, near_pairs, bfly_weights, partner_local):
    vectors, blocks, _, entries, columns = basis.shape
    size = lax.axis_size("rows")
    half = blocks // 2
    width = columns // CHUNKS
    scale = 1.0 / (size * blocks * entries)
    local_levels = blocks.bit_length() - 1
    shape = jax.ShapeDtypeStruct
    weights_spec = lambda level: pl.BlockSpec(
        (1, blocks, 4, entries, entries), lambda _: (level, 0, 0, 0, 0)
    )
    last_spec = pl.BlockSpec((1, blocks, 2, entries, columns), lambda _: (vectors - 1, 0, 0, 0, 0))

    info = jnp.pad(
        near_pairs[OWN:].astype(BF16)[:, None, :], ((0, 0), (0, 15), (0, entries - 2))
    )
    payload = jnp.concatenate(
        [near_blocks[OWN:].reshape(-1, 2 * entries, entries), info], axis=1
    )
    shipped = lax.all_gather(payload, "rows", axis=0, tiled=True)
    shipped_pairs = shipped[:, 2 * entries, :2].astype(jnp.int32)

    low, high, *sections = call(
        prep_kernel,
        [shape((half, 2 * entries, columns), BF16)] * 2
        + [shape((blocks, 2 * entries, width), BF16)] * CHUNKS,
        [SMEM, last_spec, pl.BlockSpec((2, blocks, 4, entries, entries), lambda _: (0, 0, 0, 0, 0))],
        [pltpu.VMEM((blocks, 2 * entries, columns), BF16)] * 2,
        flops=2 * 16 * blocks * entries * entries * columns,
        bytes_accessed=2**21,
    )(partner_local, basis, bfly_weights)
    before = shifted(high, 1)
    after = shifted(low, -1)

    gram_rows = vectors * vectors
    gram = call(
        functools.partial(gram_kernel, scale),
        shape((gram_rows, columns), F32),
        [VMEM],
        flops=2**23,
        bytes_accessed=2**22,
    )(basis)

    bases = call(
        near_own_kernel,
        [shape((blocks, 2 * entries, width), F32)] * CHUNKS,
        [SMEM, pl.BlockSpec((OWN, 2, entries, entries), lambda _: (0, 0, 0, 0))]
        + [VMEM] * 4
        + [last_spec],
        [
            pltpu.VMEM((2 * blocks, 2 * entries, columns), BF16),
            pltpu.VMEM((blocks, 2 * entries, columns), F32),
        ],
        flops=OWN * 8 * entries * entries * columns,
        bytes_accessed=2**22,
    )(near_pairs, near_blocks, before, low, high, after, basis)

    bases = call(
        near_shipped_kernel,
        [shape((blocks, 2 * entries, width), F32)] * CHUNKS,
        [SMEM] + [VMEM] * (5 + CHUNKS),
        [pltpu.VMEM((2 * blocks, 2 * entries, columns), BF16)],
        flops=2**28,
        bytes_accessed=2**23,
    )(shipped_pairs, shipped, before, low, high, after, *bases)

    for level in range(local_levels, LEVELS - 1):
        mask = 2 ** (level - local_levels)
        sections = [
            call(
                functools.partial(level_kernel, level),
                shape((blocks, 2 * entries, width), BF16),
                [SMEM, VMEM, VMEM, weights_spec(level)],
                flops=16 * blocks * entries * entries * width,
                bytes_accessed=2**20,
            )(partner_local, section, swapped(section, mask), bfly_weights)
            for section in sections
        ]
    level = LEVELS - 1
    mask = 2 ** (level - local_levels)
    stat_rows = -(-(2 * vectors + 1 + gram_rows) // 8) * 8
    products, stats = [], []
    for c, section in enumerate(sections):
        product, stat = call(
            functools.partial(project_kernel, level, scale),
            [shape((blocks, 2 * entries, width), F32), shape((stat_rows, width), F32)],
            [
                SMEM,
                VMEM,
                VMEM,
                weights_spec(level),
                VMEM,
                pl.BlockSpec(
                    (vectors, blocks, 2, entries, width), lambda _, c=c: (0, 0, 0, 0, c)
                ),
                pl.BlockSpec((gram_rows, width), lambda _, c=c: (0, c)),
            ],
            flops=16 * blocks * entries * entries * width,
            bytes_accessed=2**21,
        )(partner_local, section, swapped(section, mask), bfly_weights, bases[c], basis, gram)
        products.append(product)
        stats.append(stat)
    stats = jnp.concatenate(stats, axis=1)
    shared = lax.all_gather(stats, "rows", axis=0)
    following, coeffs = call(
        finish_kernel,
        [
            shape((blocks, 2, entries, columns), F32),
            shape((vectors + 1, 2, columns), F32),
        ],
        [VMEM] * (2 + CHUNKS),
        flops=2**23,
        bytes_accessed=2**23,
    )(shared, basis, *products)
    return following, coeffs


def solution(mesh):
    placed = (
        P("freq", "rows", None, None, None),
        P("rows", "freq", None, None),
        P("rows", None),
        P("freq", "rows", None, None, None),
        P(None, "rows"),
    )
    return jax.shard_map(
        shards,
        mesh=mesh,
        in_specs=placed,
        out_specs=(P("rows", "freq", None, None), P("freq", None, None)),
        check_vma=False,
    )
```

```python
import functools

import jax
import jax.numpy as jnp
from jax import lax
from jax.experimental import pallas as pl
from jax.experimental.pallas import tpu as pltpu
from jax.sharding import PartitionSpec as P

LEVELS = 6
REACH = 2
OWN = 28
CHUNKS = 2
F32 = jnp.float32
BF16 = jnp.bfloat16
VMEM = pl.BlockSpec(memory_space=pltpu.VMEM)
SMEM = pl.BlockSpec(memory_space=pltpu.SMEM)
HBM = pl.BlockSpec(memory_space=pltpu.HBM)
ANY = pl.BlockSpec(memory_space=pl.ANY)
EXTRA = 32
INFO = 8
BIG = 60
RING, NEAR, HALO = ("ring", 0), ("near", 0), ("halo", 0)
PLAN = [(3, 0), HALO, (3, 1), RING, NEAR, RING, (4, 0), RING, (4, 1)]
COSTLY = 2 * 10**10


def call(kernel, outs, in_specs, scratch=(), limit=16, after=(), cost=1):
    run = pl.pallas_call(
        kernel,
        out_shape=outs,
        in_specs=list(in_specs) + [ANY] * len(after),
        out_specs=jax.tree.map(lambda _: VMEM, outs),
        scratch_shapes=list(scratch),
        compiler_params=pltpu.CompilerParams(vmem_limit_bytes=limit * 2**20),
        cost_estimate=pl.CostEstimate(flops=cost, bytes_accessed=1, transcendentals=0),
    )
    return lambda *operands: run(*operands, *after)


def mixed(weights, own, picked):
    ur, ui, wr, wi = weights[0], weights[1], weights[2], weights[3]
    real = jnp.concatenate([ur, -ui, wr, -wi], axis=1)
    imag = jnp.concatenate([ui, ur, wi, wr], axis=1)
    left = jnp.concatenate([real, imag], axis=0)
    right = jnp.concatenate([own, picked], axis=0)
    return jnp.dot(left, right, preferred_element_type=F32)


def near_term(zr, zi, vector):
    left = jnp.concatenate(
        [jnp.concatenate([zr, -zi], axis=1), jnp.concatenate([zi, zr], axis=1)], axis=0
    )
    return jnp.dot(left, vector, preferred_element_type=F32)


def gather_kernel(scale, pairs, blocks, source, *rest):
    out, basis, gram, slot_sem, basis_sem = rest[-5:]
    count, rows, lanes = out.shape
    entries = (rows - EXTRA) // 2
    vectors, nblocks = basis.shape[0], basis.shape[1]
    columns = basis.shape[-1]
    copies = [
        pltpu.make_async_copy(source.at[:, b], basis.at[:, b], basis_sem.at[b])
        for b in range(nblocks)
    ]
    get_slots = [
        pltpu.make_async_copy(
            blocks.at[OWN + k, part],
            out.at[k, pl.ds(part * entries, entries)],
            slot_sem.at[k, part],
        )
        for k in range(count)
        for part in range(2)
    ]
    for copy in copies + get_slots:
        copy.start()
    gram[...] = jnp.zeros_like(gram)
    for b, copy in enumerate(copies):
        copy.wait()
        at = 0
        for i in range(vectors):
            ir, ii = basis[i, b, 0], basis[i, b, 1]
            for j in range(i, vectors):
                jr, ji = basis[j, b, 0], basis[j, b, 1]
                gram[at : at + 1] += jnp.sum(ir * jr + ii * ji, axis=0, keepdims=True) * scale
                at += 1
                if i != j:
                    gram[at : at + 1] += jnp.sum(ir * ji - ii * jr, axis=0, keepdims=True) * scale
                    at += 1
    whole = jnp.concatenate(
        [gram[:, c * lanes : (c + 1) * lanes] for c in range(columns // lanes)], axis=0
    )
    top = whole.astype(BF16).astype(F32)
    middle = (whole - top).astype(BF16).astype(F32)
    parts = jnp.concatenate([top, middle, whole - top - middle], axis=0)
    share = parts.shape[0] // count
    lane = lax.broadcasted_iota(jnp.int32, (INFO, lanes), 1)
    for k in range(count):
        place = jnp.where(lane == 0, pairs[0, OWN + k], jnp.where(lane == 1, pairs[1, OWN + k], 0))
        tile = [parts[k * share : (k + 1) * share], place.astype(F32)]
        out[k, 2 * entries :] = jnp.concatenate(tile, axis=0).astype(BF16)
    for copy in get_slots:
        copy.wait()


def prep_kernel(partner, basis, all_weights, low, high, *rest):
    sections, (last, weights, zero, one, last_sem, weight_sem) = rest[:-6], rest[-6:]
    blocks = last.shape[0]
    half = blocks // 2
    get_last = [
        pltpu.make_async_copy(basis.at[basis.shape[0] - 1, b], last.at[b], last_sem.at[b])
        for b in range(blocks)
    ]
    get_weights = [
        pltpu.make_async_copy(all_weights.at[level], weights.at[level], weight_sem.at[level])
        for level in range(2)
    ]
    for copy in get_last:
        copy.start()
    for copy in get_weights:
        copy.start()
    for b in range(blocks):
        get_last[b].wait()
        zero[b] = last[b].reshape(zero.shape[1:]).astype(BF16)
    low[...] = zero[:half]
    high[...] = zero[half:]
    get_weights[0].wait()
    for b in range(blocks):
        one[b] = mixed(weights[0, b], zero[b], zero[partner[b, 0]]).astype(BF16)
    get_weights[1].wait()
    for b in range(blocks):
        done = mixed(weights[1, b], one[b], one[partner[b, 1]]).astype(BF16)
        width = done.shape[1] // len(sections)
        for c, section in enumerate(sections):
            section[b] = done[:, c * width : (c + 1) * width]


def level_kernel(level, partner, own, far, weights, *rest):
    out = rest[-1]
    for b in range(own.shape[0]):
        out[b] = mixed(weights[level, b], own[b], far[partner[b, level]]).astype(BF16)


def near_own_kernel(pairs, near_blocks, before, low, high, after, basis, *rest):
    outs = rest[-6 - CHUNKS : -6]
    window, total, blocks, window_sem, last_sem, block_sem = rest[-6:]
    rows, _, entries, columns = total.shape
    half = rows // 2
    group = OWN // block_sem.shape[0]
    copies = [
        pltpu.make_async_copy(part, window.at[pl.ds(k * half, half)], window_sem.at[k])
        for k, part in enumerate((before, low, high, after))
    ]
    copies.append(pltpu.make_async_copy(basis.at[basis.shape[0] - 1], total, last_sem))
    get_blocks = [
        pltpu.make_async_copy(
            near_blocks.at[pl.ds(g * group, group)],
            blocks.at[pl.ds(g * group, group)],
            block_sem.at[g],
        )
        for g in range(block_sem.shape[0])
    ]
    for copy in copies + get_blocks:
        copy.start()
    for copy in copies:
        copy.wait()
    first = lax.axis_index("rows") * rows

    for g, copy in enumerate(get_blocks):
        copy.wait()
        for slot in range(g * group, (g + 1) * group):
            row = pairs[0, slot] - first
            col = pairs[1, slot] - first + REACH
            term = near_term(blocks[slot, 0], blocks[slot, 1], window[col])
            total[row] += term.reshape(2, entries, columns)
    width = columns // len(outs)
    for c, out in enumerate(outs):
        for b in range(rows):
            out[b] = total[b, :, :, c * width : (c + 1) * width].reshape(2 * entries, width)


def slot_offset(shipped, away, flip, skip):
    device = lax.axis_index("rows")
    chips = lax.axis_size("rows") // 2
    chip, core = device // 2, device % 2
    chip = lax.rem(chip + away * (2 * core - 1) + 2 * chips, chips)
    return (chip * 2 + (core ^ flip)) * shipped + skip


def near_shipped_kernel(places, shares, shipped, before, low, high, after, *rest):
    count = len(places)
    pieces = rest[:count]
    totals = rest[count : count + CHUNKS]
    scratch = 8 if shares else 7
    window, blocks, table, pairs, window_sem, piece_sem, table_sem = rest[-7:]
    outs = rest[-scratch - 1 - CHUNKS : -scratch - 1] if shares else rest[-7 - CHUNKS : -7]
    rows, _, width = totals[0].shape
    half = rows // 2
    entries = (blocks.shape[1] - EXTRA) // 2
    copies = [
        pltpu.make_async_copy(part, window.at[pl.ds(k * half, half)], window_sem.at[k])
        for k, part in enumerate((before, low, high, after))
    ]
    used = 0
    for k, (piece, (away, flip, start, size, skip, whole)) in enumerate(zip(pieces, places)):
        if whole:
            copies.append(
                pltpu.make_async_copy(
                    piece.at[pl.ds(start, size)], blocks.at[pl.ds(used, size)], piece_sem.at[k]
                )
            )
            used += size
        if shares:
            at = slot_offset(shipped, away, flip, skip)
            copies.append(
                pltpu.make_async_copy(
                    piece.at[pl.ds(start, size), pl.ds(2 * entries, EXTRA)],
                    rest[-8].at[pl.ds(at, size)],
                    piece_sem.at[count + k],
                )
            )
    for copy in copies:
        copy.start()
    first = lax.axis_index("rows") * rows
    for out, total in zip(outs, totals):
        out[...] = total[...]
    for copy in copies:
        copy.wait()
    below = blocks[:, 2 * entries + EXTRA - INFO :].astype(F32)
    table[...] = jnp.max(below, axis=1).astype(jnp.int32)
    copy = pltpu.make_async_copy(table, pairs, table_sem)
    copy.start()
    if shares:
        gram, below = rest[-9], rest[-8][:, : EXTRA - INFO].astype(F32)
        parts = []
        for k in range(shipped):
            part = below[k]
            for d in range(1, below.shape[0] // shipped):
                part = part + below[d * shipped + k]
            parts.append(part)
        parts = jnp.concatenate(parts, axis=0)
        whole = parts.shape[0] // 3
        parts = parts[:whole] + (parts[whole : 2 * whole] + parts[2 * whole :])
        lanes, high_rows = parts.shape[1], gram.shape[0]
        for c in range(gram.shape[1] // lanes):
            gram[:, c * lanes : (c + 1) * lanes] = parts[c * high_rows : (c + 1) * high_rows]
    copy.wait()

    def body(slot, carry):
        row = pairs[slot, 0] - first
        col = pairs[slot, 1] - first + REACH

        @pl.when((row >= 0) & (row < rows))
        def _():
            term = near_term(
                blocks[slot, 0:entries], blocks[slot, entries : 2 * entries], window[col]
            )
            for c, out in enumerate(outs):
                out[row] += term[:, c * width : (c + 1) * width]

        return carry

    lax.fori_loop(0, used, body, 0)


def project_kernel(level, chunk, scale, partner, own, far, weights, base, basis, *rest):
    product, stats = rest[-2:]
    vectors, blocks = basis.shape[0], basis.shape[1]
    entries = basis.shape[3]
    width = own.shape[2]
    cols = slice(chunk * width, (chunk + 1) * width)
    sums = [0.0] * (2 * vectors + 1)
    for b in range(blocks):
        section = mixed(weights[level, b], own[b], far[partner[b, level]]).astype(BF16)
        here = base[b] + section.astype(F32)
        product[b] = here
        pr, pi = here[:entries], here[entries:]
        for j in range(vectors):
            br, bi = basis[j, b, 0, :, cols], basis[j, b, 1, :, cols]
            sums[j] += jnp.sum(br * pr + bi * pi, axis=0, keepdims=True)
            sums[vectors + j] += jnp.sum(br * pi - bi * pr, axis=0, keepdims=True)
        sums[-1] += jnp.sum(pr * pr + pi * pi, axis=0, keepdims=True)
    for k, value in enumerate(sums):
        stats[k : k + 1] = value * scale


def finish_kernel(shared, gram, basis, *rest):
    products, (following, coeffs) = rest[:-2], rest[-2:]
    vectors, blocks = basis.shape[0], basis.shape[1]
    entries = basis.shape[3]
    total = shared[0]
    for k in range(1, shared.shape[0]):
        total = total + shared[k]
    each = 2 * vectors + 1
    whole = [
        jnp.concatenate([total[c * each + k : c * each + k + 1] for c in range(len(products))], axis=1)
        for k in range(each)
    ]
    hr, hi, square = whole[:vectors], whole[vectors : 2 * vectors], whole[-1]
    at = 0
    for i in range(vectors):
        for j in range(i, vectors):
            gr = gram[at : at + 1]
            at += 1
            if i == j:
                square = square + (gr - 2.0) * (hr[i] * hr[i] + hi[i] * hi[i])
            else:
                gi = gram[at : at + 1]
                at += 1
                square = square + 2.0 * (
                    gr * (hr[i] * hr[j] + hi[i] * hi[j]) - gi * (hr[i] * hi[j] - hi[i] * hr[j])
                )
    norm = jnp.sqrt(jnp.maximum(square, 0.0) + 1e-06)
    inverse = 1.0 / norm
    for j in range(vectors):
        coeffs[j, 0:1] = hr[j]
        coeffs[j, 1:2] = hi[j]
    coeffs[vectors, 0:1] = norm
    coeffs[vectors, 1:2] = jnp.zeros_like(norm)
    width = products[0].shape[2]
    for c, product in enumerate(products):
        cols = slice(c * width, (c + 1) * width)
        for b in range(blocks):
            real, imag = product[b, :entries], product[b, entries:]
            for j in range(vectors):
                br, bi = basis[j, b, 0, :, cols], basis[j, b, 1, :, cols]
                real = real - (br * hr[j][:, cols] - bi * hi[j][:, cols])
                imag = imag - (br * hi[j][:, cols] + bi * hr[j][:, cols])
            following[b, 0, :, cols] = real * inverse[:, cols]
            following[b, 1, :, cols] = imag * inverse[:, cols]


def swapped(value, mask):
    return lax.ppermute(value, "rows", [(i, i ^ mask) for i in range(lax.axis_size("rows"))])


def shifted(value, step):
    size = lax.axis_size("rows")
    return lax.ppermute(value, "rows", [(i, (i + step) % size) for i in range(size)])


def around(value):
    size = lax.axis_size("rows")
    return lax.ppermute(
        value, "rows", [(i, (i + (2 if i % 2 == 0 else -2)) % size) for i in range(size)]
    )


def behind(value, *others):
    return lax.optimization_barrier((value,) + others)[0]


def shards(basis, near_blocks, near_pairs, bfly_weights, partner_local):
    vectors, blocks, _, entries, columns = basis.shape
    size = lax.axis_size("rows")
    chips = size // 2
    half = blocks // 2
    width = columns // CHUNKS
    shipped = near_pairs.shape[0] - OWN
    scale = 1.0 / (size * blocks * entries)
    local_levels = blocks.bit_length() - 1
    shape = jax.ShapeDtypeStruct
    dma = pltpu.SemaphoreType.DMA
    pairs = near_pairs.T
    partner = partner_local.T

    low, high, *sections = call(
        prep_kernel,
        [shape((half, 2 * entries, columns), BF16)] * 2
        + [shape((blocks, 2 * entries, width), BF16)] * CHUNKS,
        [SMEM, HBM, HBM],
        [
            pltpu.VMEM((blocks, 2, entries, columns), F32),
            pltpu.VMEM((2, blocks, 4, entries, entries), BF16),
            pltpu.VMEM((blocks, 2 * entries, columns), BF16),
            pltpu.VMEM((blocks, 2 * entries, columns), BF16),
            dma((blocks,)),
            dma((2,)),
        ],
        limit=BIG,
    )(partner, basis, bfly_weights)

    def exchanged(level, c):
        return swapped(sections[c], 2 ** (level - local_levels))

    def level_step(level, c, far, *after):
        return call(
            functools.partial(level_kernel, level),
            shape((blocks, 2 * entries, width), BF16),
            [SMEM, VMEM, VMEM, VMEM],
            after=after,
            cost=COSTLY,
        )(partner, sections[c], far, bfly_weights)

    far = [exchanged(local_levels, c) for c in range(CHUNKS)]
    order = sections[0] = level_step(local_levels, 0, far[0])
    far[0] = exchanged(local_levels + 1, 0)

    gram_rows = vectors * vectors
    own_slots, held = call(
        functools.partial(gather_kernel, scale),
        [shape((shipped, 2 * entries + EXTRA, entries), BF16), shape(basis.shape, F32)],
        [SMEM, HBM, HBM],
        [pltpu.VMEM((gram_rows, columns), F32), dma((shipped, 2)), dma((blocks,))],
        after=(order,),
        cost=COSTLY,
    )(pairs, near_blocks, basis)
    other_slots = swapped(own_slots, 1)

    order = own_slots
    for c in range(1, CHUNKS):
        order = sections[c] = level_step(local_levels, c, far[c], order)
        far[c] = exchanged(local_levels + 1, c)

    steps = chips // 2
    order = behind(jnp.concatenate([own_slots, other_slots], axis=0), order)
    pieces, theirs = [around(order)], []
    theirs.append(swapped(pieces[0], 1))

    def ring_step(order):
        piece = behind(pieces[-1], order, *theirs[:-1])
        if len(pieces) < steps - 1:
            pieces.append(around(piece))
            theirs.append(swapped(pieces[-1], 1))
        else:
            pieces.append(around(piece[:shipped]))
        return piece

    for level, c in PLAN:
        if level == "ring":
            order = ring_step(order)
        elif level == "halo":
            before = shifted(behind(high, order), 1)
            after = shifted(behind(low, order), -1)
        elif level == "near":
            bases = call(
                near_own_kernel,
                [shape((blocks, 2 * entries, width), F32)] * CHUNKS,
                [SMEM, HBM] + [ANY] * 4 + [HBM],
                [
                    pltpu.VMEM((2 * blocks, 2 * entries, columns), BF16),
                    pltpu.VMEM((blocks, 2, entries, columns), F32),
                    pltpu.VMEM((OWN, 2, entries, entries), BF16),
                    dma((4,)),
                    dma,
                    dma((4,)),
                ],
                after=(order,),
                cost=COSTLY,
            )(pairs, near_blocks, before, low, high, after, basis)
            order = bases[0]
        else:
            order = sections[c] = level_step(level, c, far[c], order)
            far[c] = exchanged(level + 1, c)

    early = [(own_slots, (0, 0, 0, shipped, 0)), (other_slots, (0, 1, 0, shipped, 0))]
    for k in range(steps - 1):
        for flip in range(2):
            part = flip * shipped
            early.append((pieces[k], (k + 1, flip, part, shipped, 0)))
            early.append((theirs[k], (-(k + 1), 1 - flip, part, shipped, 0)))
    def near_shipped(sources, others, order, bases):
        shares = len(others) > 0
        used = sum(place[3] for _, place in sources)
        places = [place + (True,) for _, place in sources] + [place + (False,) for _, place in others]
        every = [source for source, _ in sources + others]
        return call(
            functools.partial(near_shipped_kernel, places, shares, shipped),
            [shape((blocks, 2 * entries, width), F32)] * CHUNKS
            + [shape((gram_rows, columns), F32)] * shares,
            [ANY] * (4 + len(every)) + [VMEM] * CHUNKS,
            [pltpu.VMEM((size * shipped, EXTRA, entries), BF16)] * shares
            + [
                pltpu.VMEM((2 * blocks, 2 * entries, columns), BF16),
                pltpu.VMEM((used, 2 * entries + EXTRA, entries), BF16),
                pltpu.VMEM((used, entries), jnp.int32),
                pltpu.SMEM((used, entries), jnp.int32),
                dma((4,)),
                dma((2 * len(every),)),
                dma,
            ],
            after=(order,),
        )(before, low, high, after, *every, *bases)

    bases = near_shipped(early, [], order, bases)
    late = [(pieces[-1], (steps, 0, 0, shipped, 0))]
    for k, part in enumerate(jnp.split(behind(pieces[-1], bases[0]), 2)):
        late.append((swapped(part, 1), (steps, 1, 0, shipped // 2, k * (shipped // 2))))
    *bases, gram = near_shipped(late, early, far[0], bases)

    level = LEVELS - 1
    each = 2 * vectors + 1
    products, stats = [], []
    for c in range(CHUNKS):
        product, stat = call(
            functools.partial(project_kernel, level, c, scale),
            [shape((blocks, 2 * entries, width), F32), shape((each, width), F32)],
            [SMEM] + [VMEM] * 5,
            after=tuple(stats),
        )(partner, sections[c], far[c], bfly_weights, bases[c], held)
        products.append(product)
        stats.append(stat)
    stats = jnp.concatenate(stats, axis=0)
    shared = lax.all_to_all(jnp.broadcast_to(stats, (size,) + stats.shape), "rows", 0, 0)
    following, coeffs = call(
        finish_kernel,
        [
            shape((blocks, 2, entries, columns), F32),
            shape((vectors + 1, 2, columns), F32),
        ],
        [VMEM] * (3 + CHUNKS),
    )(shared, gram, held, *products)
    return following, coeffs


def solution(mesh):
    placed = (
        P("freq", "rows", None, None, None),
        P("rows", "freq", None, None),
        P("rows", None),
        P("freq", "rows", None, None, None),
        P(None, "rows"),
    )
    return jax.shard_map(
        shards,
        mesh=mesh,
        in_specs=placed,
        out_specs=(P("rows", "freq", None, None), P("freq", None, None)),
        check_vma=False,
    )
```

```python
import functools

import jax
import jax.numpy as jnp
from jax import lax
from jax.experimental import pallas as pl
from jax.experimental.pallas import tpu as pltpu
from jax.sharding import PartitionSpec as P

LEVELS = 6
REACH = 2
OWN = 28
CHUNKS = 2
F32 = jnp.float32
BF16 = jnp.bfloat16
VMEM = pl.BlockSpec(memory_space=pltpu.VMEM)
SMEM = pl.BlockSpec(memory_space=pltpu.SMEM)
HBM = pl.BlockSpec(memory_space=pltpu.HBM)
ANY = pl.BlockSpec(memory_space=pl.ANY)
EXTRA = 32
INFO = 8
BIG = 60
GATHER = 52
EARLY = False
RING, NEAR, HALO = ("ring", 0), ("near", 0), ("halo", 0)
PLAN = [(3, 0), RING, HALO, (3, 1), NEAR, RING, (4, 0), RING, (4, 1)]
COSTLY = 2 * 10**10


def call(kernel, outs, in_specs, scratch=(), limit=16, after=(), cost=1):
    run = pl.pallas_call(
        kernel,
        out_shape=outs,
        in_specs=list(in_specs) + [ANY] * len(after),
        out_specs=jax.tree.map(lambda _: VMEM, outs),
        scratch_shapes=list(scratch),
        compiler_params=pltpu.CompilerParams(vmem_limit_bytes=limit * 2**20),
        cost_estimate=pl.CostEstimate(flops=cost, bytes_accessed=1, transcendentals=0),
    )
    return lambda *operands: run(*operands, *after)


def mixed(weights, own, picked):
    ur, ui, wr, wi = weights[0], weights[1], weights[2], weights[3]
    real = jnp.concatenate([ur, -ui, wr, -wi], axis=1)
    imag = jnp.concatenate([ui, ur, wi, wr], axis=1)
    left = jnp.concatenate([real, imag], axis=0)
    right = jnp.concatenate([own, picked], axis=0)
    return jnp.dot(left, right, preferred_element_type=F32)


def near_term(zr, zi, vector):
    left = jnp.concatenate(
        [jnp.concatenate([zr, -zi], axis=1), jnp.concatenate([zi, zr], axis=1)], axis=0
    )
    return jnp.dot(left, vector, preferred_element_type=F32)


def gather_kernel(scale, pairs, blocks, source, *rest):
    out, gram, basis, slot_sem, basis_sem = rest[-5:]
    count, rows, lanes = out.shape
    entries = (rows - EXTRA) // 2
    vectors, nblocks = basis.shape[0], basis.shape[1]
    columns = basis.shape[-1]
    copies = [
        pltpu.make_async_copy(source.at[:, b], basis.at[:, b], basis_sem.at[b])
        for b in range(nblocks)
    ]
    get_slots = [
        pltpu.make_async_copy(
            blocks.at[OWN + k, part],
            out.at[k, pl.ds(part * entries, entries)],
            slot_sem.at[k, part],
        )
        for k in range(count)
        for part in range(2)
    ]
    for copy in copies + get_slots:
        copy.start()
    gram[...] = jnp.zeros_like(gram)
    for b, copy in enumerate(copies):
        copy.wait()
        at = 0
        for i in range(vectors):
            ir, ii = basis[i, b, 0], basis[i, b, 1]
            for j in range(i, vectors):
                jr, ji = basis[j, b, 0], basis[j, b, 1]
                gram[at : at + 1] += jnp.sum(ir * jr + ii * ji, axis=0, keepdims=True) * scale
                at += 1
                if i != j:
                    gram[at : at + 1] += jnp.sum(ir * ji - ii * jr, axis=0, keepdims=True) * scale
                    at += 1
    whole = jnp.concatenate(
        [gram[:, c * lanes : (c + 1) * lanes] for c in range(columns // lanes)], axis=0
    )
    top = whole.astype(BF16).astype(F32)
    middle = (whole - top).astype(BF16).astype(F32)
    parts = jnp.concatenate([top, middle, whole - top - middle], axis=0)
    share = parts.shape[0] // count
    lane = lax.broadcasted_iota(jnp.int32, (INFO, lanes), 1)
    for k in range(count):
        place = jnp.where(lane == 0, pairs[0, OWN + k], jnp.where(lane == 1, pairs[1, OWN + k], 0))
        tile = [parts[k * share : (k + 1) * share], place.astype(F32)]
        out[k, 2 * entries :] = jnp.concatenate(tile, axis=0).astype(BF16)
    for copy in get_slots:
        copy.wait()


def prep_kernel(partner, basis, all_weights, low, high, *rest):
    sections, (last, weights, zero, one, last_sem, weight_sem) = rest[:-6], rest[-6:]
    blocks = last.shape[0]
    half = blocks // 2
    get_last = [
        pltpu.make_async_copy(basis.at[basis.shape[0] - 1, b], last.at[b], last_sem.at[b])
        for b in range(blocks)
    ]
    get_weights = [
        pltpu.make_async_copy(all_weights.at[level], weights.at[level], weight_sem.at[level])
        for level in range(2)
    ]
    for copy in get_last:
        copy.start()
    for copy in get_weights:
        copy.start()
    for b in range(blocks):
        get_last[b].wait()
        zero[b] = last[b].reshape(zero.shape[1:]).astype(BF16)
    low[...] = zero[:half]
    high[...] = zero[half:]
    get_weights[0].wait()
    for b in range(blocks):
        one[b] = mixed(weights[0, b], zero[b], zero[partner[b, 0]]).astype(BF16)
    get_weights[1].wait()
    for b in range(blocks):
        done = mixed(weights[1, b], one[b], one[partner[b, 1]]).astype(BF16)
        width = done.shape[1] // len(sections)
        for c, section in enumerate(sections):
            section[b] = done[:, c * width : (c + 1) * width]


def level_kernel(level, partner, own, far, weights, *rest):
    out = rest[-1]
    for b in range(own.shape[0]):
        out[b] = mixed(weights[level, b], own[b], far[partner[b, level]]).astype(BF16)


def near_own_kernel(pairs, near_blocks, before, low, high, after, basis, *rest):
    outs = rest[-6 - CHUNKS : -6]
    window, total, blocks, window_sem, last_sem, block_sem = rest[-6:]
    rows, _, entries, columns = total.shape
    half = rows // 2
    group = OWN // block_sem.shape[0]
    copies = [
        pltpu.make_async_copy(part, window.at[pl.ds(k * half, half)], window_sem.at[k])
        for k, part in enumerate((before, low, high, after))
    ]
    copies.append(pltpu.make_async_copy(basis.at[basis.shape[0] - 1], total, last_sem))
    get_blocks = [
        pltpu.make_async_copy(
            near_blocks.at[pl.ds(g * group, group)],
            blocks.at[pl.ds(g * group, group)],
            block_sem.at[g],
        )
        for g in range(block_sem.shape[0])
    ]
    for copy in copies + get_blocks:
        copy.start()
    for copy in copies:
        copy.wait()
    first = lax.axis_index("rows") * rows

    for g, copy in enumerate(get_blocks):
        copy.wait()
        for slot in range(g * group, (g + 1) * group):
            row = pairs[0, slot] - first
            col = pairs[1, slot] - first + REACH
            term = near_term(blocks[slot, 0], blocks[slot, 1], window[col])
            total[row] += term.reshape(2, entries, columns)
    width = columns // len(outs)
    for c, out in enumerate(outs):
        for b in range(rows):
            out[b] = total[b, :, :, c * width : (c + 1) * width].reshape(2 * entries, width)


def slot_offset(shipped, away, flip, skip):
    device = lax.axis_index("rows")
    chips = lax.axis_size("rows") // 2
    chip, core = device // 2, device % 2
    chip = lax.rem(chip + away * (2 * core - 1) + 2 * chips, chips)
    return (chip * 2 + (core ^ flip)) * shipped + skip


def near_shipped_kernel(places, shares, shipped, before, low, high, after, *rest):
    count = len(places)
    pieces = rest[:count]
    totals = rest[count : count + CHUNKS]
    scratch = 8 if shares else 7
    window, blocks, table, pairs, window_sem, piece_sem, table_sem = rest[-7:]
    outs = rest[-scratch - 1 - CHUNKS : -scratch - 1] if shares else rest[-7 - CHUNKS : -7]
    rows, _, width = totals[0].shape
    half = rows // 2
    entries = (blocks.shape[1] - EXTRA) // 2
    copies = [
        pltpu.make_async_copy(part, window.at[pl.ds(k * half, half)], window_sem.at[k])
        for k, part in enumerate((before, low, high, after))
    ]
    used = 0
    for k, (piece, (away, flip, start, size, skip, whole)) in enumerate(zip(pieces, places)):
        if whole:
            copies.append(
                pltpu.make_async_copy(
                    piece.at[pl.ds(start, size)], blocks.at[pl.ds(used, size)], piece_sem.at[k]
                )
            )
            used += size
        if shares:
            at = slot_offset(shipped, away, flip, skip)
            copies.append(
                pltpu.make_async_copy(
                    piece.at[pl.ds(start, size), pl.ds(2 * entries, EXTRA)],
                    rest[-8].at[pl.ds(at, size)],
                    piece_sem.at[count + k],
                )
            )
    for copy in copies:
        copy.start()
    first = lax.axis_index("rows") * rows
    for out, total in zip(outs, totals):
        out[...] = total[...]
    for copy in copies:
        copy.wait()
    below = blocks[:, 2 * entries + EXTRA - INFO :].astype(F32)
    table[...] = jnp.max(below, axis=1).astype(jnp.int32)
    copy = pltpu.make_async_copy(table, pairs, table_sem)
    copy.start()
    if shares:
        gram, below = rest[-9], rest[-8][:, : EXTRA - INFO].astype(F32)
        parts = []
        for k in range(shipped):
            part = below[k]
            for d in range(1, below.shape[0] // shipped):
                part = part + below[d * shipped + k]
            parts.append(part)
        parts = jnp.concatenate(parts, axis=0)
        whole = parts.shape[0] // 3
        parts = parts[:whole] + (parts[whole : 2 * whole] + parts[2 * whole :])
        lanes, high_rows = parts.shape[1], gram.shape[0]
        for c in range(gram.shape[1] // lanes):
            gram[:, c * lanes : (c + 1) * lanes] = parts[c * high_rows : (c + 1) * high_rows]
    copy.wait()

    def body(slot, carry):
        row = pairs[slot, 0] - first
        col = pairs[slot, 1] - first + REACH

        @pl.when((row >= 0) & (row < rows))
        def _():
            term = near_term(
                blocks[slot, 0:entries], blocks[slot, entries : 2 * entries], window[col]
            )
            for c, out in enumerate(outs):
                out[row] += term[:, c * width : (c + 1) * width]

        return carry

    lax.fori_loop(0, used, body, 0)


def hold_kernel(source, *rest):
    held, sem = rest[-2:]
    copy = pltpu.make_async_copy(source, held, sem)
    copy.start()
    copy.wait()


def project_kernel(level, chunk, scale, partner, own, far, weights, base, basis, *rest):
    product, stats = rest[-2:]
    vectors, blocks = basis.shape[0], basis.shape[1]
    entries = basis.shape[3]
    width = own.shape[2]
    cols = slice(chunk * width, (chunk + 1) * width)
    sums = [0.0] * (2 * vectors + 1)
    for b in range(blocks):
        section = mixed(weights[level, b], own[b], far[partner[b, level]]).astype(BF16)
        here = base[b] + section.astype(F32)
        product[b] = here
        pr, pi = here[:entries], here[entries:]
        for j in range(vectors):
            br, bi = basis[j, b, 0, :, cols], basis[j, b, 1, :, cols]
            sums[j] += jnp.sum(br * pr + bi * pi, axis=0, keepdims=True)
            sums[vectors + j] += jnp.sum(br * pi - bi * pr, axis=0, keepdims=True)
        sums[-1] += jnp.sum(pr * pr + pi * pi, axis=0, keepdims=True)
    for k, value in enumerate(sums):
        stats[k : k + 1] = value * scale


def finish_kernel(shared, gram, basis, *rest):
    products, (following, coeffs) = rest[:-2], rest[-2:]
    vectors, blocks = basis.shape[0], basis.shape[1]
    entries = basis.shape[3]
    total = shared[0]
    for k in range(1, shared.shape[0]):
        total = total + shared[k]
    each = 2 * vectors + 1
    whole = [
        jnp.concatenate([total[c * each + k : c * each + k + 1] for c in range(len(products))], axis=1)
        for k in range(each)
    ]
    hr, hi, square = whole[:vectors], whole[vectors : 2 * vectors], whole[-1]
    at = 0
    for i in range(vectors):
        for j in range(i, vectors):
            gr = gram[at : at + 1]
            at += 1
            if i == j:
                square = square + (gr - 2.0) * (hr[i] * hr[i] + hi[i] * hi[i])
            else:
                gi = gram[at : at + 1]
                at += 1
                square = square + 2.0 * (
                    gr * (hr[i] * hr[j] + hi[i] * hi[j]) - gi * (hr[i] * hi[j] - hi[i] * hr[j])
                )
    norm = jnp.sqrt(jnp.maximum(square, 0.0) + 1e-06)
    inverse = 1.0 / norm
    for j in range(vectors):
        coeffs[j, 0:1] = hr[j]
        coeffs[j, 1:2] = hi[j]
    coeffs[vectors, 0:1] = norm
    coeffs[vectors, 1:2] = jnp.zeros_like(norm)
    width = products[0].shape[2]
    for c, product in enumerate(products):
        cols = slice(c * width, (c + 1) * width)
        for b in range(blocks):
            real, imag = product[b, :entries], product[b, entries:]
            for j in range(vectors):
                br, bi = basis[j, b, 0, :, cols], basis[j, b, 1, :, cols]
                real = real - (br * hr[j][:, cols] - bi * hi[j][:, cols])
                imag = imag - (br * hi[j][:, cols] + bi * hr[j][:, cols])
            following[b, 0, :, cols] = real * inverse[:, cols]
            following[b, 1, :, cols] = imag * inverse[:, cols]


def swapped(value, mask):
    return lax.ppermute(value, "rows", [(i, i ^ mask) for i in range(lax.axis_size("rows"))])


def shifted(value, step):
    size = lax.axis_size("rows")
    return lax.ppermute(value, "rows", [(i, (i + step) % size) for i in range(size)])


def around(value):
    size = lax.axis_size("rows")
    return lax.ppermute(
        value, "rows", [(i, (i + (2 if i % 2 == 0 else -2)) % size) for i in range(size)]
    )


def behind(value, *others):
    return lax.optimization_barrier((value,) + others)[0]


def shards(basis, near_blocks, near_pairs, bfly_weights, partner_local):
    vectors, blocks, _, entries, columns = basis.shape
    size = lax.axis_size("rows")
    chips = size // 2
    half = blocks // 2
    width = columns // CHUNKS
    shipped = near_pairs.shape[0] - OWN
    scale = 1.0 / (size * blocks * entries)
    local_levels = blocks.bit_length() - 1
    shape = jax.ShapeDtypeStruct
    dma = pltpu.SemaphoreType.DMA
    pairs = near_pairs.T
    partner = partner_local.T

    low, high, *sections = call(
        prep_kernel,
        [shape((half, 2 * entries, columns), BF16)] * 2
        + [shape((blocks, 2 * entries, width), BF16)] * CHUNKS,
        [SMEM, HBM, HBM],
        [
            pltpu.VMEM((blocks, 2, entries, columns), F32),
            pltpu.VMEM((2, blocks, 4, entries, entries), BF16),
            pltpu.VMEM((blocks, 2 * entries, columns), BF16),
            pltpu.VMEM((blocks, 2 * entries, columns), BF16),
            dma((blocks,)),
            dma((2,)),
        ],
        limit=BIG,
    )(partner, basis, bfly_weights)

    def exchanged(level, c):
        return swapped(sections[c], 2 ** (level - local_levels))

    def level_step(level, c, far, *after):
        return call(
            functools.partial(level_kernel, level),
            shape((blocks, 2 * entries, width), BF16),
            [SMEM, VMEM, VMEM, VMEM],
            after=after,
            cost=COSTLY,
        )(partner, sections[c], far, bfly_weights)

    far = [exchanged(local_levels, c) for c in range(CHUNKS)]
    order = sections[0] = level_step(local_levels, 0, far[0])
    far[0] = exchanged(local_levels + 1, 0)

    gram_rows = vectors * vectors
    own_slots = call(
        functools.partial(gather_kernel, scale),
        shape((shipped, 2 * entries + EXTRA, entries), BF16),
        [SMEM, HBM, HBM],
        [
            pltpu.VMEM((gram_rows, columns), F32),
            pltpu.VMEM(basis.shape, F32),
            dma((shipped, 2)),
            dma((blocks,)),
        ],
        after=(order,),
        cost=COSTLY,
        limit=GATHER,
    )(pairs, near_blocks, basis)
    other_slots = swapped(own_slots, 1)

    order = own_slots

    steps = chips // 2
    if EARLY:
        order = behind(jnp.concatenate([own_slots, other_slots], axis=0), order)
        pieces, theirs = [around(order)], []
        theirs.append(swapped(pieces[0], 1))
    for c in range(1, CHUNKS):
        order = sections[c] = level_step(local_levels, c, far[c], order)
        far[c] = exchanged(local_levels + 1, c)
    if not EARLY:
        order = behind(jnp.concatenate([own_slots, other_slots], axis=0), order)
        pieces, theirs = [around(order)], []
        theirs.append(swapped(pieces[0], 1))

    def ring_step(order):
        piece = behind(pieces[-1], order, *theirs[:-1])
        if len(pieces) < steps - 1:
            pieces.append(around(piece))
            theirs.append(swapped(pieces[-1], 1))
        else:
            pieces.append(around(piece[:shipped]))
        return piece

    for level, c in PLAN:
        if level == "ring":
            order = ring_step(order)
        elif level == "halo":
            before = shifted(behind(high, order), 1)
            after = shifted(behind(low, order), -1)
        elif level == "near":
            bases = call(
                near_own_kernel,
                [shape((blocks, 2 * entries, width), F32)] * CHUNKS,
                [SMEM, HBM] + [ANY] * 4 + [HBM],
                [
                    pltpu.VMEM((2 * blocks, 2 * entries, columns), BF16),
                    pltpu.VMEM((blocks, 2, entries, columns), F32),
                    pltpu.VMEM((OWN, 2, entries, entries), BF16),
                    dma((4,)),
                    dma,
                    dma((4,)),
                ],
                after=(order,),
                cost=COSTLY,
            )(pairs, near_blocks, before, low, high, after, basis)
            held = call(
                hold_kernel, shape(basis.shape, F32), [HBM], [dma], after=(bases[0],), cost=COSTLY
            )(basis)
            order = held
        else:
            order = sections[c] = level_step(level, c, far[c], order)
            far[c] = exchanged(level + 1, c)

    early = [(own_slots, (0, 0, 0, shipped, 0)), (other_slots, (0, 1, 0, shipped, 0))]
    for k in range(steps - 1):
        for flip in range(2):
            part = flip * shipped
            early.append((pieces[k], (k + 1, flip, part, shipped, 0)))
            early.append((theirs[k], (-(k + 1), 1 - flip, part, shipped, 0)))
    def near_shipped(sources, others, order, bases):
        shares = len(others) > 0
        used = sum(place[3] for _, place in sources)
        places = [place + (True,) for _, place in sources] + [place + (False,) for _, place in others]
        every = [source for source, _ in sources + others]
        return call(
            functools.partial(near_shipped_kernel, places, shares, shipped),
            [shape((blocks, 2 * entries, width), F32)] * CHUNKS
            + [shape((gram_rows, columns), F32)] * shares,
            [ANY] * (4 + len(every)) + [VMEM] * CHUNKS,
            [pltpu.VMEM((size * shipped, EXTRA, entries), BF16)] * shares
            + [
                pltpu.VMEM((2 * blocks, 2 * entries, columns), BF16),
                pltpu.VMEM((used, 2 * entries + EXTRA, entries), BF16),
                pltpu.VMEM((used, entries), jnp.int32),
                pltpu.SMEM((used, entries), jnp.int32),
                dma((4,)),
                dma((2 * len(every),)),
                dma,
            ],
            after=(order,),
        )(before, low, high, after, *every, *bases)

    bases = near_shipped(early, [], order, bases)
    late = [(pieces[-1], (steps, 0, 0, shipped, 0))]
    for k, part in enumerate(jnp.split(behind(pieces[-1], bases[0]), 2)):
        late.append((swapped(part, 1), (steps, 1, 0, shipped // 2, k * (shipped // 2))))
    *bases, gram = near_shipped(late, early, far[0], bases)

    level = LEVELS - 1
    each = 2 * vectors + 1
    products, stats = [], []
    for c in range(CHUNKS):
        product, stat = call(
            functools.partial(project_kernel, level, c, scale),
            [shape((blocks, 2 * entries, width), F32), shape((each, width), F32)],
            [SMEM] + [VMEM] * 5,
            after=tuple(stats),
        )(partner, sections[c], far[c], bfly_weights, bases[c], held)
        products.append(product)
        stats.append(stat)
    stats = jnp.concatenate(stats, axis=0)
    shared = lax.all_to_all(jnp.broadcast_to(stats, (size,) + stats.shape), "rows", 0, 0)
    following, coeffs = call(
        finish_kernel,
        [
            shape((blocks, 2, entries, columns), F32),
            shape((vectors + 1, 2, columns), F32),
        ],
        [VMEM] * (3 + CHUNKS),
    )(shared, gram, held, *products)
    return following, coeffs


def solution(mesh):
    placed = (
        P("freq", "rows", None, None, None),
        P("rows", "freq", None, None),
        P("rows", None),
        P("freq", "rows", None, None, None),
        P(None, "rows"),
    )
    return jax.shard_map(
        shards,
        mesh=mesh,
        in_specs=placed,
        out_specs=(P("rows", "freq", None, None), P("freq", None, None)),
        check_vma=False,
    )
```
